32 devices in a mesh: row: 4 (over y, x), col: 8 (over z, core).
Axes of the slice: x: 2, y: 2, z: 4, core: 2. Of those that a mesh axis runs over, the one named last changes fastest.
Arguments:
- sigma_anc: bfloat16 [1024, 1024], P('row', 'col'), as said below
- structure: int32 [32, 4], P(('row', 'col')), may hold values from 0 to 3, all different within a row
- factor: bfloat16 [32, 1024, 1024], P(('row', 'col')), may hold values from -0.375 to 0.375
- diag_term: float32 [32, 1024], P(('row', 'col')), may hold values from 1 to 8
Outputs:
- sigma_off: bfloat16 [32, 1024, 1024], P(('row', 'col'))
- variances: float32 [32, 1024], P(('row', 'col'))
The draws below stay inside these ranges and needn't reach their ends.
Inputs may be any that keep to these rules, and one draw needn't show every extreme that they name: `structure`: each row names 4 different ancestor blocks, and every ancestor block is named by some row. sigma_anc is exactly symmetric, as the inverse of a symmetric precision matrix: its entry (p, q) equals its entry (q, p) bit for bit.
All inputs are finite; a program needn't handle non-finite values.
Results may differ from the reference program's by a relative error of at most 0.001.
Values may be sent and summed in bfloat16 or wider, within the bound.
A program may use at most 64 MiB of HBM per device.

```python
import math
import jax
import jax.numpy as jnp
from jax import lax

B = 256
W = 1024
S = 4
NA = 4
NS = 32


def draw_sigma_anc(key, part):
    total = NA * B
    first_key, second_key = jax.random.split(jax.random.fold_in(key, 17))
    raw_values = jax.random.normal(first_key, (total, total), jnp.float32)
    diagonal_values = jax.random.uniform(second_key, (total,), jnp.float32, 1.0, 2.0)
    symmetric = (raw_values + raw_values.T) * (0.7071 / total ** 0.5)
    return (symmetric + jnp.diag(diagonal_values)).astype(jnp.bfloat16)


def block_scale(own_key, shape, pieces, smallest, largest):
    loudness = 1.0
    for dim, shards_of in pieces:
        draws = jax.random.uniform(jax.random.fold_in(jax.random.fold_in(own_key, 6), dim), (shards_of,), jnp.float32, smallest / len(pieces), largest / len(pieces))
        loudness = loudness * jnp.repeat(jnp.exp(draws), shape[dim] // shards_of).reshape((-1,) + (1,) * (len(shape) - 1 - dim))
    return loudness


def distinct(rng, rows, amount, top, lift):
    sequence = jax.random.permutation(jax.random.fold_in(rng, 1), amount)
    favour = sequence
    for power in range(3):
        favour = favour * favour // amount
    favour = favour * lift // amount
    lots = jax.random.randint(jax.random.fold_in(rng, 2), (rows, amount), 0, 4096) + favour
    fixed_rows = jax.random.permutation(jax.random.fold_in(rng, 3), rows)[jnp.arange(amount) % rows]
    lots = jnp.where(jnp.arange(rows)[:, None] == fixed_rows[None, :], 1 << 14, lots)
    merit = lots * amount + jnp.arange(amount)
    return lax.top_k(merit.astype(jnp.int32), top)[1].astype(jnp.int32)


def noise(own_key, extent, spread, limit, shards=(), dtype=jnp.bfloat16):
    level = block_scale(own_key, extent, shards, -0.22, 0.18) if shards else 1.0
    result = jax.random.normal(own_key, extent, jnp.float32) * spread * level
    return jnp.minimum(jnp.maximum(result, -limit), limit).astype(dtype)


def setup_inputs(seed: int = 0) -> dict:
    key_list = jax.random.split(jax.random.key(seed), 5)
    sigma_anc = draw_sigma_anc(jax.random.fold_in(key_list[4], 71), 0)
    structure = distinct(key_list[1], NS, NA, S, 12000)
    factor = noise(key_list[2], (NS, S * B, W), (S * B // 4) ** -0.5, 0.375, ((0, 32),))
    diag_term = jnp.clip(jnp.exp(math.log(8.0) - 2.0794415 * jax.random.uniform(key_list[3], (NS, W), jnp.float32) ** block_scale(key_list[3], (NS, W), ((0, 32),), -0.2, 0.2)), 1.0, 8.0)
    return dict(sigma_anc=sigma_anc, structure=structure, factor=factor, diag_term=diag_term)


def reference(sigma_anc, structure, factor, diag_term):
    block_total = sigma_anc.shape[0] // B
    blocked = sigma_anc.reshape(block_total, B, block_total, B)

    def single(inputs):
        own_blocks, triangle, diag_row = inputs
        picked_rows = jnp.take(blocked, own_blocks, axis=0)
        gram_block = jnp.take(picked_rows, own_blocks, axis=2).reshape(S * B, S * B)
        product = -jnp.dot(gram_block, triangle, preferred_element_type=jnp.float32)
        variance = diag_row - jnp.sum(triangle.astype(jnp.float32) * product, axis=0)
        return product.astype(jnp.bfloat16), variance

    sigma_off, variances = lax.map(single, (structure, factor, diag_term))
    return sigma_off, variances
```

```python
import functools

import jax
import jax.numpy as jnp
from jax import lax
from jax.experimental import pallas as pl
from jax.experimental.pallas import tpu as pltpu
from jax.sharding import PartitionSpec as P

MESH = pl.DeviceIdType.MESH
OWN, ALONG_X, ALONG_Y, ACROSS = range(4)


def flip(value, mask):
    bit = 1
    while bit <= mask:
        if mask & bit:
            value = value + bit - 2 * bit * ((value // bit) % 2)
        bit *= 2
    return value


def kernel(
    planes,
    sigma_ref,
    structure_ref,
    factor_ref,
    diag_ref,
    out_ref,
    var_ref,
    held,
    gram,
    tri,
    result,
    local_sem,
    out_sem,
    line_send,
    line_recv,
    pair_send,
    pair_recv,
    core_send,
    core_recv,
):
    row = lax.axis_index("row")
    col = lax.axis_index("col")
    plane, core = col // 2, col % 2
    half = sigma_ref.shape[1]
    spans = structure_ref.shape[1]
    block = factor_ref.shape[0] // spans
    width = factor_ref.shape[1]

    load_factor = pltpu.make_async_copy(factor_ref, tri, local_sem.at[0])
    load_factor.start()
    keep_low = pltpu.make_async_copy(sigma_ref.at[pl.ds(0, half)], held.at[row, col, 0], local_sem.at[1])
    keep_high = pltpu.make_async_copy(sigma_ref.at[pl.ds(half, half)], held.at[row, col, 1], local_sem.at[2])
    keep_low.start()
    keep_high.start()

    sibling = (row, flip(col, 1))
    beside = {e: (flip(row, e), col) for e in (ALONG_X, ALONG_Y)}
    line = {s: (row, flip(plane, s) * 2 + core) for s in range(1, planes)}
    greeted = [sibling, *beside.values(), *line.values()]
    barrier = pltpu.get_barrier_semaphore()
    for device in greeted:
        pl.semaphore_signal(barrier, inc=1, device_id=device, device_id_type=MESH)
    pl.semaphore_wait(barrier, len(greeted))

    def piece(e, s, which, extra):
        rr, zz = flip(row, e), flip(plane, s)
        h = jnp.where(rr > zz, 1 - which, which)
        return held.at[rr, zz * 2 + which, 1 - h if extra else h]

    def both(e, s, act):
        act(0)

        @pl.when(flip(row, e) == flip(plane, s))
        def _():
            act(1)

    def copy(e, s, extra, device, send, recv, landing, first=False):
        which = core if landing is None else landing
        source = piece(e, s, which, extra)
        target = source
        if first:
            h = jnp.where(row > plane, 1 - core, core)
            h = 1 - h if extra else h
            source = sigma_ref.at[pl.ds(pl.multiple_of(h * half, half), half)]
        return pltpu.make_async_remote_copy(
            src_ref=source, dst_ref=target, send_sem=send.at[extra], recv_sem=recv.at[extra],
            device_id=device, device_id_type=MESH)

    pending = []

    def post(e, s, device, send, recv, first=False):
        both(e, s, lambda extra: copy(e, s, extra, device, send, recv, None, first).start())
        pending.append((e, s, device, send, recv, first))

    def arrive(e, s, device, send, recv, which=None):
        both(e, s, lambda extra: copy(e, s, extra, device, send, recv, which).wait_recv())

    def to_line(s):
        post(OWN, 0, line[s], line_send.at[s], line_recv.at[s], True)

    def to_pair(e, s, via, kind, first=False):
        post(e, s, beside[via], pair_send.at[kind, s], pair_recv.at[kind, s], first)

    def to_core(e, s, first=False):
        post(e, s, sibling, core_send.at[e, s], core_recv.at[e, s], first)

    def from_pair(e, s):
        arrive(e, s, beside[ALONG_X], pair_send.at[e, s], pair_recv.at[e, s])

    def spread(s):
        from_pair(ALONG_X, s)
        if s % 2 == 0:
            to_pair(ALONG_X, s, ALONG_Y, ACROSS)
        to_core(ALONG_X, s)
        from_pair(ALONG_Y, s)
        if s % 2 == 1:
            to_pair(ALONG_Y, s, ALONG_X, ACROSS)
        to_core(ALONG_Y, s)

    to_pair(OWN, 0, ALONG_X, ALONG_X, True)
    to_pair(OWN, 0, ALONG_Y, ALONG_Y, True)
    for s in range(1, planes):
        to_line(s)
    to_core(OWN, 0, True)

    for s in range(1, planes):
        arrive(OWN, s, line[s], line_send.at[s], line_recv.at[s])
        to_pair(OWN, s, ALONG_X, ALONG_X)
        to_pair(OWN, s, ALONG_Y, ALONG_Y)
        to_core(OWN, s)
        spread(s - 1)
    spread(planes - 1)

    load_factor.wait()
    for s in range(planes):
        from_pair(ACROSS, s)
        to_core(ACROSS, s)
    keep_low.wait()
    keep_high.wait()
    for e in range(spans):
        for s in range(planes):
            arrive(e, s, sibling, core_send.at[e, s], core_recv.at[e, s], 1 - core)

    def put(p, q, a, b, value):
        gram[p, q, a * half:(a + 1) * half, b * half:(b + 1) * half] = value

    for p in range(spans):
        for a in range(2):
            for b in range(2):
                put(p, p, a, b, held[p, 2 * p + b, a])
        for q in range(p + 1, spans):
            for a in range(2):
                upper = held[p, 2 * q + a, a]
                put(p, q, a, a, upper)
                put(q, p, a, a, upper.T)
                lower = held[q, 2 * p + a, 1 - a]
                put(q, p, 1 - a, a, lower)
                put(p, q, a, 1 - a, lower.T)

    tile = block
    steps = width // tile

    def out_copy(n):
        cols = pl.ds(pl.multiple_of(n * tile, tile), tile)
        return pltpu.make_async_copy(result.at[:, cols], out_ref.at[:, cols], out_sem.at[n])

    def step(n, _):
        cols = pl.ds(pl.multiple_of(n * tile, tile), tile)
        total = jnp.zeros((1, tile), jnp.float32)
        for i in range(spans):
            own = jnp.concatenate([gram[structure_ref[0, i], structure_ref[0, m]] for m in range(spans)], axis=1)
            product = -jnp.dot(own, tri[:, cols], preferred_element_type=jnp.float32)
            result[i * block:(i + 1) * block, cols] = product.astype(jnp.bfloat16)
            total += jnp.sum(tri[i * block:(i + 1) * block, cols].astype(jnp.float32) * product, axis=0, keepdims=True)
        var_ref[:, cols] = diag_ref[:, cols] - total
        out_copy(n).start()
        return 0

    lax.fori_loop(0, steps, step, 0)
    for n in range(steps):
        out_copy(n).wait()
    for e, s, device, send, recv, first in pending:
        both(e, s, lambda extra: copy(e, s, extra, device, send, recv, None, first).wait_send())


def gathered(planes, sigma_anc, structure, factor, diag_term):
    rows, half = sigma_anc.shape
    spans = structure.shape[1]
    depth, width = factor.shape[1:]
    anywhere = pl.BlockSpec(memory_space=pl.ANY)
    in_vmem = pl.BlockSpec(memory_space=pltpu.VMEM)
    dma = pltpu.SemaphoreType.DMA
    off, variance = pl.pallas_call(
        functools.partial(kernel, planes),
        out_shape=(
            jax.ShapeDtypeStruct((depth, width), jnp.bfloat16),
            jax.ShapeDtypeStruct((1, width), jnp.float32),
        ),
        in_specs=[anywhere, pl.BlockSpec(memory_space=pltpu.SMEM), anywhere, in_vmem],
        out_specs=(anywhere, in_vmem),
        scratch_shapes=[
            pltpu.VMEM((spans, 2 * planes, 2, half, half), jnp.bfloat16),
            pltpu.VMEM((spans, spans, 2 * half, 2 * half), jnp.bfloat16),
            pltpu.VMEM((depth, width), jnp.bfloat16),
            pltpu.VMEM((depth, width), jnp.bfloat16),
            dma((3,)),
            dma((spans,)),
            dma((planes, 2)),
            dma((planes, 2)),
            dma((4, planes, 2)),
            dma((4, planes, 2)),
            dma((4, planes, 2)),
            dma((4, planes, 2)),
        ],
        compiler_params=pltpu.CompilerParams(
            collective_id=0, has_side_effects=True, vmem_limit_bytes=48 * 1024 * 1024
        ),
        cost_estimate=pl.CostEstimate(
            flops=2 * depth * depth * width, bytes_accessed=4 * depth * width, transcendentals=0
        ),
    )(sigma_anc, structure, factor[0], diag_term)
    return off[None], variance


def selected(sigma_anc, structure, factor, diag_term):
    span_count = structure.shape[1]
    block_rows = factor.shape[1] // span_count
    own_blocks = structure[0]
    triangle = factor[0]
    panel = lax.all_gather(sigma_anc, "col", axis=1, tiled=True)
    structures = lax.all_gather(structure, "row", axis=0, tiled=True)
    block_total = panel.shape[1] // block_rows
    blocked = panel.reshape(block_rows, block_total, block_rows)
    outgoing = jnp.take(blocked, structures, axis=1)
    outgoing = outgoing.reshape(block_rows, structures.shape[0], span_count * block_rows)
    received = lax.all_to_all(outgoing, "row", split_axis=1, concat_axis=1, tiled=True)
    picked = jnp.take(received, own_blocks, axis=1)
    product = jnp.einsum("bim,mw->ibw", picked, triangle, preferred_element_type=jnp.float32)
    off_block = -product.reshape(span_count * block_rows, triangle.shape[1])
    variance = diag_term[0] - jnp.sum(triangle.astype(jnp.float32) * off_block, axis=0)
    return (off_block.astype(jnp.bfloat16)[None], variance[None])


def solution(mesh):
    rows, planes = mesh.shape["row"], mesh.shape["col"] // 2

    def body(sigma_anc, structure, factor, diag_term):
        spans = structure.shape[1]
        if rows == spans == planes == ACROSS + 1 and sigma_anc.shape[0] == 2 * sigma_anc.shape[1]:
            return gathered(planes, sigma_anc, structure, factor, diag_term)
        return selected(sigma_anc, structure, factor, diag_term)

    return jax.shard_map(
        body,
        mesh=mesh,
        in_specs=(
            P("row", "col"),
            P(("row", "col"), None),
            P(("row", "col"), None, None),
            P(("row", "col"), None),
        ),
        out_specs=(P(("row", "col"), None, None), P(("row", "col"), None)),
        check_vma=False,
    )
```

```python
import functools

import jax
import jax.numpy as jnp
from jax import lax
from jax.experimental import pallas as pl
from jax.experimental.pallas import tpu as pltpu
from jax.sharding import PartitionSpec as P

MESH = pl.DeviceIdType.MESH
OWN, ALONG_X, ALONG_Y, ACROSS = range(4)


def flip(value, mask):
    bit = 1
    while bit <= mask:
        if mask & bit:
            value = value + bit - 2 * bit * ((value // bit) % 2)
        bit *= 2
    return value


def kernel(
    planes,
    sigma_ref,
    structure_ref,
    factor_ref,
    diag_ref,
    out_ref,
    var_ref,
    held,
    gram,
    tri,
    result,
    blocks,
    diag,
    local_sem,
    out_sem,
    send_sem,
    extra_sem,
    line_sem,
    pair_sem,
    core_sem,
):
    row = lax.axis_index("row")
    col = lax.axis_index("col")
    plane, core = col // 2, col % 2
    half = sigma_ref.shape[1]
    spans = structure_ref.shape[1]
    block = factor_ref.shape[0] // spans
    width = factor_ref.shape[1]

    def take(h):
        return sigma_ref.at[pl.ds(pl.multiple_of(h * half, half), half)]

    main = take(jnp.where(row > plane, 1 - core, core))
    extra = take(1 - core)
    on_diagonal = row == plane

    keep = pltpu.make_async_copy(main, held.at[0, 0, 0], local_sem.at[0])
    keep_extra = pltpu.make_async_copy(extra, held.at[0, 0, planes], local_sem.at[1])
    load_factor = pltpu.make_async_copy(factor_ref, tri, local_sem.at[2])
    load_blocks = pltpu.make_async_copy(structure_ref, blocks, local_sem.at[3])
    load_diag = pltpu.make_async_copy(diag_ref, diag, local_sem.at[4])
    keep.start()
    pl.when(on_diagonal)(keep_extra.start)

    sibling = (row, col + 1 - 2 * core)
    beside = {e: (flip(row, e), col) for e in (ALONG_X, ALONG_Y)}
    line = {s: (row, flip(plane, s) * 2 + core) for s in range(1, planes)}
    greeted = [*line.values(), *beside.values(), sibling]
    barrier = pltpu.get_barrier_semaphore()
    for device in greeted:
        pl.semaphore_signal(barrier, inc=1, device_id=device, device_id_type=MESH)
    load_factor.start()
    load_blocks.start()
    load_diag.start()
    pl.semaphore_wait(barrier, len(greeted))

    sent = []

    def remote(source, target, recv, device, send=send_sem):
        return pltpu.make_async_remote_copy(
            src_ref=source, dst_ref=target, send_sem=send, recv_sem=recv,
            device_id=device, device_id_type=MESH)

    def to_line(s):
        remote(main, held.at[0, 0, s], line_sem.at[s], line[s]).start()
        sent.append(1)

    def from_line(s):
        remote(held.at[0, 0, s], held.at[0, 0, s], line_sem.at[s], line[1]).wait_recv()

    def extra_to_line(s):
        return remote(extra, held.at[0, 0, planes], line_sem.at[0], line[s], extra_sem.at[s])

    def to_pair(e, via, s, source=None):
        source = held.at[e, 0, s] if source is None else source
        remote(source, held.at[e + via, 0, s], pair_sem.at[e + via, s], beside[via]).start()
        sent.append(1)

    def from_pair(e, s):
        remote(held.at[e, 0, s], held.at[e, 0, s], pair_sem.at[e, s], beside[ALONG_X]).wait_recv()

    parts = ((0, 2), (2, planes + 1))

    def to_core(e, part):
        lo, hi = parts[part]
        remote(held.at[e, 0, lo:hi], held.at[e, 1, lo:hi], core_sem.at[e, part], sibling).start()
        sent.append(hi - lo)

    def from_core(e):
        for part, (lo, hi) in enumerate(parts):
            remote(held.at[e, 1, lo:hi], held.at[e, 1, lo:hi], core_sem.at[e, part], sibling).wait_recv()

    to_pair(OWN, ALONG_X, 0, main)
    to_pair(OWN, ALONG_Y, 0, main)
    for s in range(1, planes):
        to_line(s)

    @pl.when(on_diagonal)
    def _():
        for s in range(1, planes):
            extra_to_line(s).start()

    keep.wait()
    for s in range(1, planes):
        from_line(s)
        to_pair(OWN, ALONG_X, s)
        to_pair(OWN, ALONG_Y, s)
        if s == 1:
            to_core(OWN, 0)
            from_pair(ALONG_X, 0)
            to_pair(ALONG_X, ALONG_Y, 0)
            from_pair(ALONG_Y, 0)

    @pl.when(on_diagonal)
    def _():
        keep_extra.wait()

    @pl.when(jnp.logical_not(on_diagonal))
    def _():
        extra_to_line(1).wait_recv()

    to_pair(OWN, ALONG_X, planes)
    to_pair(OWN, ALONG_Y, planes)
    to_core(OWN, 1)
    for s in range(1, planes + 1):
        from_pair(ALONG_X, s)
        if s == planes:
            to_pair(ALONG_X, ALONG_Y, s)
        from_pair(ALONG_Y, s)
        if s < planes:
            to_pair(ALONG_Y, ALONG_X, s)
        if s == 1:
            to_core(ALONG_X, 0)
            to_core(ALONG_Y, 0)
    to_core(ALONG_X, 1)
    to_core(ALONG_Y, 1)

    differ, bit = 0, 1
    while bit < planes:
        one, two = (row // bit) % 2, (plane // bit) % 2
        differ = differ + bit * (one + two - 2 * one * two)
        bit *= 2
    at_row = [flip(row, e) for e in range(spans)]
    at_plane = [flip(differ, e) for e in range(spans)]

    def put(p, q, a, b, value):
        gram[p, q, a * half:(a + 1) * half, b * half:(b + 1) * half] = value

    def other(which):
        return which + core - 2 * which * core

    def diagonal(e):
        p = at_row[e]
        for which in range(2):
            put(p, p, which, which, held[e, other(which), at_plane[e]])
            put(p, p, 1 - which, which, held[e, other(which), planes])

    def off_diagonal(e, f):
        up = at_row[e] < at_row[f]
        lo, hi = jnp.where(up, e, f), jnp.where(up, f, e)
        p, q = jnp.where(up, at_row[e], at_row[f]), jnp.where(up, at_row[f], at_row[e])
        p_plane, q_plane = jnp.where(up, at_plane[e], at_plane[f]), jnp.where(up, at_plane[f], at_plane[e])
        for which in range(2):
            upper = held[lo, other(which), q_plane]
            put(p, q, which, which, upper)
            put(q, p, which, which, upper.T)
            lower = held[hi, other(which), p_plane]
            put(q, p, 1 - which, which, lower)
            put(p, q, which, 1 - which, lower.T)

    from_core(OWN)
    diagonal(OWN)
    from_core(ALONG_X)
    diagonal(ALONG_X)
    off_diagonal(OWN, ALONG_X)
    from_pair(ACROSS, 0)
    from_pair(ACROSS, 1)
    to_core(ACROSS, 0)
    from_core(ALONG_Y)
    diagonal(ALONG_Y)
    off_diagonal(OWN, ALONG_Y)
    off_diagonal(ALONG_X, ALONG_Y)
    for s in range(2, planes + 1):
        from_pair(ACROSS, s)
    to_core(ACROSS, 1)
    load_factor.wait()
    load_blocks.wait()
    load_diag.wait()
    from_core(ACROSS)
    diagonal(ACROSS)
    for e in (OWN, ALONG_X, ALONG_Y):
        off_diagonal(e, ACROSS)

    tile = block
    steps = width // tile

    def out_copy(n):
        cols = pl.ds(pl.multiple_of(n * tile, tile), tile)
        return pltpu.make_async_copy(result.at[:, cols], out_ref.at[:, cols], out_sem.at[n])

    def step(n, _):
        cols = pl.ds(pl.multiple_of(n * tile, tile), tile)
        total = jnp.zeros((1, tile), jnp.float32)
        for i in range(spans):
            own = jnp.concatenate([gram[blocks[0, i], blocks[0, m]] for m in range(spans)], axis=1)
            product = -jnp.dot(own, tri[:, cols], preferred_element_type=jnp.float32)
            result[i * block:(i + 1) * block, cols] = product.astype(jnp.bfloat16)
            total += jnp.sum(tri[i * block:(i + 1) * block, cols].astype(jnp.float32) * product, axis=0, keepdims=True)
        var_ref[:, cols] = diag[:, cols] - total
        out_copy(n).start()
        return 0

    lax.fori_loop(0, steps, step, 0)

    same_bytes = tri.at[0:sum(sent) * half * half // width]
    pltpu.make_async_copy(same_bytes, same_bytes, send_sem).wait()

    @pl.when(on_diagonal)
    def _():
        for s in range(1, planes):
            extra_to_line(s).wait_send()

    for n in range(steps):
        out_copy(n).wait()


def gathered(planes, sigma_anc, structure, factor, diag_term):
    rows, half = sigma_anc.shape
    spans = structure.shape[1]
    depth, width = factor.shape[1:]
    anywhere = pl.BlockSpec(memory_space=pl.ANY)
    in_vmem = pl.BlockSpec(memory_space=pltpu.VMEM)
    dma = pltpu.SemaphoreType.DMA
    off, variance = pl.pallas_call(
        functools.partial(kernel, planes),
        out_shape=(
            jax.ShapeDtypeStruct((depth, width), jnp.bfloat16),
            jax.ShapeDtypeStruct((1, width), jnp.float32),
        ),
        in_specs=[anywhere] * 4,
        out_specs=(anywhere, in_vmem),
        scratch_shapes=[
            pltpu.VMEM((spans, 2, planes + 1, half, half), jnp.bfloat16),
            pltpu.VMEM((spans, spans, 2 * half, 2 * half), jnp.bfloat16),
            pltpu.VMEM((depth, width), jnp.bfloat16),
            pltpu.VMEM((depth, width), jnp.bfloat16),
            pltpu.SMEM((1, spans), jnp.int32),
            pltpu.VMEM((1, width), jnp.float32),
            dma((5,)),
            dma((spans,)),
            dma(()),
            dma((planes,)),
            dma((planes,)),
            dma((spans, planes + 1)),
            dma((spans, 2)),
        ],
        compiler_params=pltpu.CompilerParams(
            collective_id=0, has_side_effects=True, vmem_limit_bytes=60 * 1024 * 1024
        ),
        cost_estimate=pl.CostEstimate(
            flops=2 * depth * depth * width, bytes_accessed=4 * depth * width, transcendentals=0
        ),
    )(sigma_anc, structure, factor[0], diag_term)
    return off[None], variance


def selected(sigma_anc, structure, factor, diag_term):
    span_count = structure.shape[1]
    block_rows = factor.shape[1] // span_count
    own_blocks = structure[0]
    triangle = factor[0]
    panel = lax.all_gather(sigma_anc, "col", axis=1, tiled=True)
    structures = lax.all_gather(structure, "row", axis=0, tiled=True)
    block_total = panel.shape[1] // block_rows
    blocked = panel.reshape(block_rows, block_total, block_rows)
    outgoing = jnp.take(blocked, structures, axis=1)
    outgoing = outgoing.reshape(block_rows, structures.shape[0], span_count * block_rows)
    received = lax.all_to_all(outgoing, "row", split_axis=1, concat_axis=1, tiled=True)
    picked = jnp.take(received, own_blocks, axis=1)
    product = jnp.einsum("bim,mw->ibw", picked, triangle, preferred_element_type=jnp.float32)
    off_block = -product.reshape(span_count * block_rows, triangle.shape[1])
    variance = diag_term[0] - jnp.sum(triangle.astype(jnp.float32) * off_block, axis=0)
    return (off_block.astype(jnp.bfloat16)[None], variance[None])


def solution(mesh):
    rows, planes = mesh.shape["row"], mesh.shape["col"] // 2

    def body(sigma_anc, structure, factor, diag_term):
        spans = structure.shape[1]
        if rows == spans == planes == ACROSS + 1 and sigma_anc.shape[0] == 2 * sigma_anc.shape[1]:
            return gathered(planes, sigma_anc, structure, factor, diag_term)
        return selected(sigma_anc, structure, factor, diag_term)

    return jax.shard_map(
        body,
        mesh=mesh,
        in_specs=(
            P("row", "col"),
            P(("row", "col"), None),
            P(("row", "col"), None, None),
            P(("row", "col"), None),
        ),
        out_specs=(P(("row", "col"), None, None), P(("row", "col"), None)),
        check_vma=False,
    )
```

```python
import functools

import jax
import jax.numpy as jnp
from jax import lax
from jax.experimental import pallas as pl
from jax.experimental.pallas import tpu as pltpu
from jax.sharding import PartitionSpec as P

MESH = pl.DeviceIdType.MESH
OWN, ALONG_X, ALONG_Y, ACROSS = range(4)


def flip(value, mask):
    bit = 1
    while bit <= mask:
        if mask & bit:
            value = value + bit - 2 * bit * ((value // bit) % 2)
        bit *= 2
    return value


def kernel(
    planes,
    sigma_ref,
    gram,
    held,
    total,
    local_sem,
    send_sem,
    extra_sem,
    line_sem,
    pair_sem,
    core_sem,
):
    row = lax.axis_index("row")
    col = lax.axis_index("col")
    plane, core = col // 2, col % 2
    half = sigma_ref.shape[1]
    spans = gram.shape[0]

    def take(h):
        return sigma_ref.at[pl.ds(pl.multiple_of(h * half, half), half)]

    main = take(jnp.where(row > plane, 1 - core, core))
    extra = take(1 - core)
    on_diagonal = row == plane

    keep = pltpu.make_async_copy(main, held.at[0, 0, 0], local_sem.at[0])
    keep_extra = pltpu.make_async_copy(extra, held.at[0, 0, planes], local_sem.at[1])
    keep.start()
    pl.when(on_diagonal)(keep_extra.start)

    sibling = (row, col + 1 - 2 * core)
    beside = {e: (flip(row, e), col) for e in (ALONG_X, ALONG_Y)}
    line = {s: (row, flip(plane, s) * 2 + core) for s in range(1, planes)}
    greeted = [*line.values(), *beside.values(), sibling]
    barrier = pltpu.get_barrier_semaphore()
    for device in greeted:
        pl.semaphore_signal(barrier, inc=1, device_id=device, device_id_type=MESH)
    pl.semaphore_wait(barrier, len(greeted))

    sent = []

    def remote(source, target, recv, device, send=send_sem):
        return pltpu.make_async_remote_copy(
            src_ref=source, dst_ref=target, send_sem=send, recv_sem=recv,
            device_id=device, device_id_type=MESH)

    def to_line(s):
        remote(main, held.at[0, 0, s], line_sem.at[s], line[s]).start()
        sent.append(1)

    def from_line(s):
        remote(held.at[0, 0, s], held.at[0, 0, s], line_sem.at[s], line[1]).wait_recv()

    def extra_to_line(s):
        return remote(extra, held.at[0, 0, planes], line_sem.at[0], line[s], extra_sem.at[s])

    def to_pair(e, via, s, source=None):
        source = held.at[e, 0, s] if source is None else source
        remote(source, held.at[e + via, 0, s], pair_sem.at[e + via, s], beside[via]).start()
        sent.append(1)

    def from_pair(e, s):
        remote(held.at[e, 0, s], held.at[e, 0, s], pair_sem.at[e, s], beside[ALONG_X]).wait_recv()

    parts = ((0, 2), (2, planes + 1))

    def to_core(e, part):
        lo, hi = parts[part]
        remote(held.at[e, 0, lo:hi], held.at[e, 1, lo:hi], core_sem.at[e, part], sibling).start()
        sent.append(hi - lo)

    def from_core(e):
        for part, (lo, hi) in enumerate(parts):
            remote(held.at[e, 1, lo:hi], held.at[e, 1, lo:hi], core_sem.at[e, part], sibling).wait_recv()

    to_pair(OWN, ALONG_X, 0, main)
    to_pair(OWN, ALONG_Y, 0, main)
    for s in range(1, planes):
        to_line(s)

    @pl.when(on_diagonal)
    def _():
        for s in range(1, planes):
            extra_to_line(s).start()

    keep.wait()
    for s in range(1, planes):
        from_line(s)
        to_pair(OWN, ALONG_X, s)
        to_pair(OWN, ALONG_Y, s)
        if s == 1:
            to_core(OWN, 0)
            from_pair(ALONG_X, 0)
            to_pair(ALONG_X, ALONG_Y, 0)
            from_pair(ALONG_Y, 0)

    @pl.when(on_diagonal)
    def _():
        keep_extra.wait()

    @pl.when(jnp.logical_not(on_diagonal))
    def _():
        extra_to_line(1).wait_recv()

    to_pair(OWN, ALONG_X, planes)
    to_pair(OWN, ALONG_Y, planes)
    to_core(OWN, 1)
    for s in range(1, planes + 1):
        from_pair(ALONG_X, s)
        if s == planes:
            to_pair(ALONG_X, ALONG_Y, s)
        from_pair(ALONG_Y, s)
        if s < planes:
            to_pair(ALONG_Y, ALONG_X, s)
        if s == 1:
            to_core(ALONG_X, 0)
            to_core(ALONG_Y, 0)
    to_core(ALONG_X, 1)
    to_core(ALONG_Y, 1)

    differ, bit = 0, 1
    while bit < planes:
        one, two = (row // bit) % 2, (plane // bit) % 2
        differ = differ + bit * (one + two - 2 * one * two)
        bit *= 2
    at_row = [flip(row, e) for e in range(spans)]
    at_plane = [flip(differ, e) for e in range(spans)]

    def put(p, q, a, b, value):
        gram[p, q, a * half:(a + 1) * half, b * half:(b + 1) * half] = value

    def other(which):
        return which + core - 2 * which * core

    def diagonal(e):
        p = at_row[e]
        for which in range(2):
            put(p, p, which, which, held[e, other(which), at_plane[e]])
            put(p, p, 1 - which, which, held[e, other(which), planes])

    def off_diagonal(e, f):
        up = at_row[e] < at_row[f]
        lo, hi = jnp.where(up, e, f), jnp.where(up, f, e)
        p, q = jnp.where(up, at_row[e], at_row[f]), jnp.where(up, at_row[f], at_row[e])
        p_plane, q_plane = jnp.where(up, at_plane[e], at_plane[f]), jnp.where(up, at_plane[f], at_plane[e])
        for which in range(2):
            upper = held[lo, other(which), q_plane]
            put(p, q, which, which, upper)
            put(q, p, which, which, upper.T)
            lower = held[hi, other(which), p_plane]
            put(q, p, 1 - which, which, lower)
            put(p, q, which, 1 - which, lower.T)

    from_core(OWN)
    diagonal(OWN)
    from_core(ALONG_X)
    diagonal(ALONG_X)
    off_diagonal(OWN, ALONG_X)
    from_pair(ACROSS, 0)
    from_pair(ACROSS, 1)
    to_core(ACROSS, 0)
    from_core(ALONG_Y)
    diagonal(ALONG_Y)
    off_diagonal(OWN, ALONG_Y)
    off_diagonal(ALONG_X, ALONG_Y)
    for s in range(2, planes + 1):
        from_pair(ACROSS, s)
    to_core(ACROSS, 1)
    from_core(ACROSS)
    diagonal(ACROSS)
    for e in (OWN, ALONG_X, ALONG_Y):
        off_diagonal(e, ACROSS)

    same_bytes = total.at[0:sum(sent)]
    pltpu.make_async_copy(same_bytes, same_bytes, send_sem).wait()

    @pl.when(on_diagonal)
    def _():
        for s in range(1, planes):
            extra_to_line(s).wait_send()


def multiply(structure_ref, gram, tri, diag_ref, out_ref, var_ref, result, out_sem):
    spans = gram.shape[0]
    block = gram.shape[2]
    width = tri.shape[1]
    tile = block
    steps = width // tile

    def out_copy(n):
        cols = pl.ds(pl.multiple_of(n * tile, tile), tile)
        return pltpu.make_async_copy(result.at[:, cols], out_ref.at[:, cols], out_sem.at[n])

    def step(n, _):
        cols = pl.ds(pl.multiple_of(n * tile, tile), tile)
        total = jnp.zeros((1, tile), jnp.float32)
        for i in range(spans):
            own = jnp.concatenate([gram[structure_ref[0, i], structure_ref[0, m]] for m in range(spans)], axis=1)
            product = -jnp.dot(own, tri[:, cols], preferred_element_type=jnp.float32)
            result[i * block:(i + 1) * block, cols] = product.astype(jnp.bfloat16)
            total += jnp.sum(tri[i * block:(i + 1) * block, cols].astype(jnp.float32) * product, axis=0, keepdims=True)
        var_ref[:, cols] = diag_ref[:, cols] - total
        out_copy(n).start()
        return 0

    lax.fori_loop(0, steps, step, 0)
    for n in range(steps):
        out_copy(n).wait()


def gathered(planes, sigma_anc, structure, factor, diag_term):
    rows, half = sigma_anc.shape
    spans = structure.shape[1]
    depth, width = factor.shape[1:]
    anywhere = pl.BlockSpec(memory_space=pl.ANY)
    in_hbm = pl.BlockSpec(memory_space=pltpu.HBM)
    in_vmem = pl.BlockSpec(memory_space=pltpu.VMEM)
    in_smem = pl.BlockSpec(memory_space=pltpu.SMEM)
    dma = pltpu.SemaphoreType.DMA
    pieces = spans * 2 * (planes + 1)
    gram = pl.pallas_call(
        functools.partial(kernel, planes),
        out_shape=jax.ShapeDtypeStruct((spans, spans, 2 * half, 2 * half), jnp.bfloat16),
        in_specs=[in_hbm],
        out_specs=in_vmem,
        scratch_shapes=[
            pltpu.VMEM((spans, 2, planes + 1, half, half), jnp.bfloat16),
            pltpu.VMEM((pieces, half, half), jnp.bfloat16),
            dma((2,)),
            dma(()),
            dma((planes,)),
            dma((planes,)),
            dma((spans, planes + 1)),
            dma((spans, 2)),
        ],
        compiler_params=pltpu.CompilerParams(
            collective_id=0, has_side_effects=True, vmem_limit_bytes=16 * 1024 * 1024
        ),
        cost_estimate=pl.CostEstimate(flops=0, bytes_accessed=16 * depth * depth, transcendentals=0),
    )(sigma_anc)
    off, variance = pl.pallas_call(
        multiply,
        out_shape=(
            jax.ShapeDtypeStruct((depth, width), jnp.bfloat16),
            jax.ShapeDtypeStruct((1, width), jnp.float32),
        ),
        in_specs=[in_smem, in_vmem, in_vmem, in_vmem],
        out_specs=(anywhere, in_vmem),
        scratch_shapes=[pltpu.VMEM((depth, width), jnp.bfloat16), dma((spans,))],
        compiler_params=pltpu.CompilerParams(vmem_limit_bytes=24 * 1024 * 1024),
        cost_estimate=pl.CostEstimate(
            flops=2 * depth * depth * width, bytes_accessed=4 * depth * width, transcendentals=0
        ),
    )(structure, gram, factor[0], diag_term)
    return off[None], variance


def selected(sigma_anc, structure, factor, diag_term):
    span_count = structure.shape[1]
    block_rows = factor.shape[1] // span_count
    own_blocks = structure[0]
    triangle = factor[0]
    panel = lax.all_gather(sigma_anc, "col", axis=1, tiled=True)
    structures = lax.all_gather(structure, "row", axis=0, tiled=True)
    block_total = panel.shape[1] // block_rows
    blocked = panel.reshape(block_rows, block_total, block_rows)
    outgoing = jnp.take(blocked, structures, axis=1)
    outgoing = outgoing.reshape(block_rows, structures.shape[0], span_count * block_rows)
    received = lax.all_to_all(outgoing, "row", split_axis=1, concat_axis=1, tiled=True)
    picked = jnp.take(received, own_blocks, axis=1)
    product = jnp.einsum("bim,mw->ibw", picked, triangle, preferred_element_type=jnp.float32)
    off_block = -product.reshape(span_count * block_rows, triangle.shape[1])
    variance = diag_term[0] - jnp.sum(triangle.astype(jnp.float32) * off_block, axis=0)
    return (off_block.astype(jnp.bfloat16)[None], variance[None])


def solution(mesh):
    rows, planes = mesh.shape["row"], mesh.shape["col"] // 2

    def body(sigma_anc, structure, factor, diag_term):
        spans = structure.shape[1]
        if rows == spans == planes == ACROSS + 1 and sigma_anc.shape[0] == 2 * sigma_anc.shape[1]:
            return gathered(planes, sigma_anc, structure, factor, diag_term)
        return selected(sigma_anc, structure, factor, diag_term)

    return jax.shard_map(
        body,
        mesh=mesh,
        in_specs=(
            P("row", "col"),
            P(("row", "col"), None),
            P(("row", "col"), None, None),
            P(("row", "col"), None),
        ),
        out_specs=(P(("row", "col"), None, None), P(("row", "col"), None)),
        check_vma=False,
    )
```

```python
import functools

import jax
import jax.numpy as jnp
from jax import lax
from jax.experimental import pallas as pl
from jax.experimental.pallas import tpu as pltpu
from jax.sharding import PartitionSpec as P

MESH = pl.DeviceIdType.MESH
OWN, ALONG_X, ALONG_Y, ACROSS = range(4)


def flip(value, mask):
    bit = 1
    while bit <= mask:
        if mask & bit:
            value = value + bit - 2 * bit * ((value // bit) % 2)
        bit *= 2
    return value


def kernel(
    planes,
    sigma_ref,
    gram,
    held,
    total,
    local_sem,
    send_sem,
    extra_sem,
    line_sem,
    pair_sem,
    core_sem,
):
    row = lax.axis_index("row")
    col = lax.axis_index("col")
    plane, core = col // 2, col % 2
    half = sigma_ref.shape[1]
    spans = gram.shape[0]

    def take(h):
        return sigma_ref.at[pl.ds(pl.multiple_of(h * half, half), half)]

    main = take(jnp.where(row > plane, 1 - core, core))
    extra = take(1 - core)
    on_diagonal = row == plane

    keep = pltpu.make_async_copy(main, held.at[0, 0, 0], local_sem.at[0])
    keep_extra = pltpu.make_async_copy(extra, held.at[0, 0, planes], local_sem.at[1])
    keep.start()
    pl.when(on_diagonal)(keep_extra.start)

    sibling = (row, col + 1 - 2 * core)
    beside = {e: (flip(row, e), col) for e in (ALONG_X, ALONG_Y)}
    line = {s: (row, flip(plane, s) * 2 + core) for s in range(1, planes)}
    greeted = [*line.values(), *beside.values(), sibling]
    barrier = pltpu.get_barrier_semaphore()
    for device in greeted:
        pl.semaphore_signal(barrier, inc=1, device_id=device, device_id_type=MESH)
    pl.semaphore_wait(barrier, len(greeted))

    sent = []

    def remote(source, target, recv, device, send=send_sem):
        return pltpu.make_async_remote_copy(
            src_ref=source, dst_ref=target, send_sem=send, recv_sem=recv,
            device_id=device, device_id_type=MESH)

    def to_line(s):
        remote(main, held.at[0, 0, s], line_sem.at[s], line[s]).start()
        sent.append(1)

    def from_line(s):
        remote(held.at[0, 0, s], held.at[0, 0, s], line_sem.at[s], line[1]).wait_recv()

    def extra_to_line(s):
        return remote(extra, held.at[0, 0, planes], line_sem.at[0], line[s], extra_sem.at[s])

    def to_pair(e, via, s, source=None):
        source = held.at[e, 0, s] if source is None else source
        remote(source, held.at[e + via, 0, s], pair_sem.at[e + via, s], beside[via]).start()
        sent.append(1)

    def from_pair(e, s):
        remote(held.at[e, 0, s], held.at[e, 0, s], pair_sem.at[e, s], beside[ALONG_X]).wait_recv()

    parts = ((0, 2), (2, planes + 1))

    def to_core(e, part):
        lo, hi = parts[part]
        remote(held.at[e, 0, lo:hi], held.at[e, 1, lo:hi], core_sem.at[e, part], sibling).start()
        sent.append(hi - lo)

    def from_core(e):
        for part, (lo, hi) in enumerate(parts):
            remote(held.at[e, 1, lo:hi], held.at[e, 1, lo:hi], core_sem.at[e, part], sibling).wait_recv()

    to_pair(OWN, ALONG_X, 0, main)
    to_pair(OWN, ALONG_Y, 0, main)
    for s in range(1, planes):
        to_line(s)

    @pl.when(on_diagonal)
    def _():
        for s in range(1, planes):
            extra_to_line(s).start()

    keep.wait()
    for s in range(1, planes):
        from_line(s)
        to_pair(OWN, ALONG_X, s)
        to_pair(OWN, ALONG_Y, s)
        if s == 1:
            to_core(OWN, 0)
            from_pair(ALONG_X, 0)
            to_pair(ALONG_X, ALONG_Y, 0)
            from_pair(ALONG_Y, 0)

    @pl.when(on_diagonal)
    def _():
        keep_extra.wait()

    @pl.when(jnp.logical_not(on_diagonal))
    def _():
        extra_to_line(1).wait_recv()

    to_pair(OWN, ALONG_X, planes)
    to_pair(OWN, ALONG_Y, planes)
    to_core(OWN, 1)
    for s in range(1, planes + 1):
        from_pair(ALONG_X, s)
        if s == planes:
            to_pair(ALONG_X, ALONG_Y, s)
        from_pair(ALONG_Y, s)
        if s < planes:
            to_pair(ALONG_Y, ALONG_X, s)
        if s == 1:
            to_core(ALONG_X, 0)
            to_core(ALONG_Y, 0)
    to_core(ALONG_X, 1)
    to_core(ALONG_Y, 1)

    differ, bit = 0, 1
    while bit < planes:
        one, two = (row // bit) % 2, (plane // bit) % 2
        differ = differ + bit * (one + two - 2 * one * two)
        bit *= 2
    at_row = [flip(row, e) for e in range(spans)]
    at_plane = [flip(differ, e) for e in range(spans)]

    def put(p, q, a, b, value):
        gram[p, q, a * half:(a + 1) * half, b * half:(b + 1) * half] = value

    def other(which):
        return which + core - 2 * which * core

    def diagonal(e):
        p = at_row[e]
        for which in range(2):
            put(p, p, which, which, held[e, other(which), at_plane[e]])
            put(p, p, 1 - which, which, held[e, other(which), planes])

    def off_diagonal(e, f):
        up = at_row[e] < at_row[f]
        lo, hi = jnp.where(up, e, f), jnp.where(up, f, e)
        p, q = jnp.where(up, at_row[e], at_row[f]), jnp.where(up, at_row[f], at_row[e])
        p_plane, q_plane = jnp.where(up, at_plane[e], at_plane[f]), jnp.where(up, at_plane[f], at_plane[e])
        for which in range(2):
            upper = held[lo, other(which), q_plane]
            put(p, q, which, which, upper)
            put(q, p, which, which, upper.T)
            lower = held[hi, other(which), p_plane]
            put(q, p, 1 - which, which, lower)
            put(p, q, which, 1 - which, lower.T)

    from_core(OWN)
    diagonal(OWN)
    from_core(ALONG_X)
    diagonal(ALONG_X)
    off_diagonal(OWN, ALONG_X)
    from_pair(ACROSS, 0)
    from_pair(ACROSS, 1)
    to_core(ACROSS, 0)
    from_core(ALONG_Y)
    diagonal(ALONG_Y)
    off_diagonal(OWN, ALONG_Y)
    off_diagonal(ALONG_X, ALONG_Y)
    for s in range(2, planes + 1):
        from_pair(ACROSS, s)
    to_core(ACROSS, 1)
    from_core(ACROSS)
    diagonal(ACROSS)
    for e in (OWN, ALONG_X, ALONG_Y):
        off_diagonal(e, ACROSS)

    same_bytes = total.at[0:sum(sent)]
    pltpu.make_async_copy(same_bytes, same_bytes, send_sem).wait()

    @pl.when(on_diagonal)
    def _():
        for s in range(1, planes):
            extra_to_line(s).wait_send()


def multiply(structure_ref, gram, tri, diag_ref, out_ref, var_ref, own, result, out_sem):
    spans = gram.shape[0]
    block = gram.shape[2]
    width = tri.shape[1]
    tile = block
    steps = width // tile

    def out_copy(n):
        cols = pl.ds(pl.multiple_of(n * tile, tile), tile)
        return pltpu.make_async_copy(result.at[:, cols], out_ref.at[:, cols], out_sem.at[n])

    for i in range(spans):
        for m in range(spans):
            own[i * block:(i + 1) * block, m * block:(m + 1) * block] = gram[structure_ref[0, i], structure_ref[0, m]]

    def step(n, _):
        cols = pl.ds(pl.multiple_of(n * tile, tile), tile)
        product = -jnp.dot(own[...], tri[:, cols], preferred_element_type=jnp.float32)
        result[:, cols] = product.astype(jnp.bfloat16)
        total = jnp.sum(tri[:, cols].astype(jnp.float32) * product, axis=0, keepdims=True)
        var_ref[:, cols] = diag_ref[:, cols] - total
        out_copy(n).start()
        return 0

    lax.fori_loop(0, steps, step, 0)
    for n in range(steps):
        out_copy(n).wait()


def gathered(planes, sigma_anc, structure, factor, diag_term):
    rows, half = sigma_anc.shape
    spans = structure.shape[1]
    depth, width = factor.shape[1:]
    anywhere = pl.BlockSpec(memory_space=pl.ANY)
    in_hbm = pl.BlockSpec(memory_space=pltpu.HBM)
    in_vmem = pl.BlockSpec(memory_space=pltpu.VMEM)
    in_smem = pl.BlockSpec(memory_space=pltpu.SMEM)
    dma = pltpu.SemaphoreType.DMA
    pieces = spans * 2 * (planes + 1)
    gram = pl.pallas_call(
        functools.partial(kernel, planes),
        out_shape=jax.ShapeDtypeStruct((spans, spans, 2 * half, 2 * half), jnp.bfloat16),
        in_specs=[in_hbm],
        out_specs=in_vmem,
        scratch_shapes=[
            pltpu.VMEM((spans, 2, planes + 1, half, half), jnp.bfloat16),
            pltpu.VMEM((pieces, half, half), jnp.bfloat16),
            dma((2,)),
            dma(()),
            dma((planes,)),
            dma((planes,)),
            dma((spans, planes + 1)),
            dma((spans, 2)),
        ],
        compiler_params=pltpu.CompilerParams(
            collective_id=0, has_side_effects=True, vmem_limit_bytes=16 * 1024 * 1024
        ),
        cost_estimate=pl.CostEstimate(flops=0, bytes_accessed=16 * depth * depth, transcendentals=0),
    )(pltpu.with_memory_space_constraint(sigma_anc, pltpu.HBM))
    off, variance = pl.pallas_call(
        multiply,
        out_shape=(
            jax.ShapeDtypeStruct((depth, width), jnp.bfloat16),
            jax.ShapeDtypeStruct((1, width), jnp.float32),
        ),
        in_specs=[in_smem, in_vmem, in_vmem, in_vmem],
        out_specs=(anywhere, in_vmem),
        scratch_shapes=[
            pltpu.VMEM((depth, depth), jnp.bfloat16),
            pltpu.VMEM((depth, width), jnp.bfloat16),
            dma((spans,)),
        ],
        compiler_params=pltpu.CompilerParams(vmem_limit_bytes=24 * 1024 * 1024),
        cost_estimate=pl.CostEstimate(
            flops=2 * depth * depth * width, bytes_accessed=4 * depth * width, transcendentals=0
        ),
    )(structure, gram, factor[0], diag_term)
    return off[None], variance


def selected(sigma_anc, structure, factor, diag_term):
    span_count = structure.shape[1]
    block_rows = factor.shape[1] // span_count
    own_blocks = structure[0]
    triangle = factor[0]
    panel = lax.all_gather(sigma_anc, "col", axis=1, tiled=True)
    structures = lax.all_gather(structure, "row", axis=0, tiled=True)
    block_total = panel.shape[1] // block_rows
    blocked = panel.reshape(block_rows, block_total, block_rows)
    outgoing = jnp.take(blocked, structures, axis=1)
    outgoing = outgoing.reshape(block_rows, structures.shape[0], span_count * block_rows)
    received = lax.all_to_all(outgoing, "row", split_axis=1, concat_axis=1, tiled=True)
    picked = jnp.take(received, own_blocks, axis=1)
    product = jnp.einsum("bim,mw->ibw", picked, triangle, preferred_element_type=jnp.float32)
    off_block = -product.reshape(span_count * block_rows, triangle.shape[1])
    variance = diag_term[0] - jnp.sum(triangle.astype(jnp.float32) * off_block, axis=0)
    return (off_block.astype(jnp.bfloat16)[None], variance[None])


def solution(mesh):
    rows, planes = mesh.shape["row"], mesh.shape["col"] // 2

    def body(sigma_anc, structure, factor, diag_term):
        spans = structure.shape[1]
        if rows == spans == planes == ACROSS + 1 and sigma_anc.shape[0] == 2 * sigma_anc.shape[1]:
            return gathered(planes, sigma_anc, structure, factor, diag_term)
        return selected(sigma_anc, structure, factor, diag_term)

    return jax.shard_map(
        body,
        mesh=mesh,
        in_specs=(
            P("row", "col"),
            P(("row", "col"), None),
            P(("row", "col"), None, None),
            P(("row", "col"), None),
        ),
        out_specs=(P(("row", "col"), None, None), P(("row", "col"), None)),
        check_vma=False,
    )
```

```python
import functools

import jax
import jax.numpy as jnp
from jax import lax
from jax.experimental import pallas as pl
from jax.experimental.pallas import tpu as pltpu
from jax.sharding import PartitionSpec as P

MESH = pl.DeviceIdType.MESH
OWN, ALONG_X, ALONG_Y, ACROSS = range(4)


def flip(value, mask):
    bit = 1
    while bit <= mask:
        if mask & bit:
            value = value + bit - 2 * bit * ((value // bit) % 2)
        bit *= 2
    return value


def kernel(
    planes,
    sigma_ref,
    gram,
    held,
    total,
    local_sem,
    send_sem,
    extra_sem,
    line_sem,
    pair_sem,
    core_sem,
):
    row = lax.axis_index("row")
    col = lax.axis_index("col")
    plane, core = col // 2, col % 2
    half = sigma_ref.shape[1]
    spans = gram.shape[0]

    def take(h):
        return sigma_ref.at[pl.ds(pl.multiple_of(h * half, half), half)]

    main = take(jnp.where(row > plane, 1 - core, core))
    extra = take(1 - core)
    on_diagonal = row == plane

    keep = pltpu.make_async_copy(main, held.at[0, 0, 0], local_sem.at[0])
    keep_extra = pltpu.make_async_copy(extra, held.at[0, 0, planes], local_sem.at[1])
    keep.start()
    pl.when(on_diagonal)(keep_extra.start)

    sibling = (row, col + 1 - 2 * core)
    beside = {e: (flip(row, e), col) for e in (ALONG_X, ALONG_Y)}
    line = {s: (row, flip(plane, s) * 2 + core) for s in range(1, planes)}
    greeted = [*line.values(), *beside.values(), sibling]
    barrier = pltpu.get_barrier_semaphore()
    for device in greeted:
        pl.semaphore_signal(barrier, inc=1, device_id=device, device_id_type=MESH)
    pl.semaphore_wait(barrier, len(greeted))

    sent = []

    def remote(source, target, recv, device, send=send_sem):
        return pltpu.make_async_remote_copy(
            src_ref=source, dst_ref=target, send_sem=send, recv_sem=recv,
            device_id=device, device_id_type=MESH)

    def to_line(s):
        remote(main, held.at[0, 0, s], line_sem.at[s], line[s]).start()
        sent.append(1)

    def from_line(s):
        remote(held.at[0, 0, s], held.at[0, 0, s], line_sem.at[s], line[1]).wait_recv()

    def extra_to_line(s):
        return remote(extra, held.at[0, 0, planes], line_sem.at[0], line[s], extra_sem.at[s])

    def to_pair(e, via, s, source=None):
        source = held.at[e, 0, s] if source is None else source
        remote(source, held.at[e + via, 0, s], pair_sem.at[e + via, s], beside[via]).start()
        sent.append(1)

    def from_pair(e, s):
        remote(held.at[e, 0, s], held.at[e, 0, s], pair_sem.at[e, s], beside[ALONG_X]).wait_recv()

    parts = ((0, 2), (2, planes + 1))

    def to_core(e, part):
        lo, hi = parts[part]
        remote(held.at[e, 0, lo:hi], held.at[e, 1, lo:hi], core_sem.at[e, part], sibling).start()
        sent.append(hi - lo)

    def from_core(e):
        for part, (lo, hi) in enumerate(parts):
            remote(held.at[e, 1, lo:hi], held.at[e, 1, lo:hi], core_sem.at[e, part], sibling).wait_recv()

    to_pair(OWN, ALONG_X, 0, main)
    to_pair(OWN, ALONG_Y, 0, main)
    for s in range(1, planes):
        to_line(s)

    @pl.when(on_diagonal)
    def _():
        for s in range(1, planes):
            extra_to_line(s).start()

    keep.wait()
    for s in range(1, planes):
        from_line(s)
        to_pair(OWN, ALONG_X, s)
        to_pair(OWN, ALONG_Y, s)
        if s == 1:
            to_core(OWN, 0)
            from_pair(ALONG_X, 0)
            to_pair(ALONG_X, ALONG_Y, 0)
            from_pair(ALONG_Y, 0)

    @pl.when(on_diagonal)
    def _():
        keep_extra.wait()

    @pl.when(jnp.logical_not(on_diagonal))
    def _():
        extra_to_line(1).wait_recv()

    to_pair(OWN, ALONG_X, planes)
    to_pair(OWN, ALONG_Y, planes)
    to_core(OWN, 1)
    for s in range(1, planes + 1):
        from_pair(ALONG_X, s)
        if s == planes:
            to_pair(ALONG_X, ALONG_Y, s)
        from_pair(ALONG_Y, s)
        if s < planes:
            to_pair(ALONG_Y, ALONG_X, s)
        if s == 1:
            to_core(ALONG_X, 0)
            to_core(ALONG_Y, 0)
    to_core(ALONG_X, 1)
    to_core(ALONG_Y, 1)

    differ, bit = 0, 1
    while bit < planes:
        one, two = (row // bit) % 2, (plane // bit) % 2
        differ = differ + bit * (one + two - 2 * one * two)
        bit *= 2
    at_row = [flip(row, e) for e in range(spans)]
    at_plane = [flip(differ, e) for e in range(spans)]

    def put(p, q, a, b, value):
        gram[p, q, a * half:(a + 1) * half, b * half:(b + 1) * half] = value

    def other(which):
        return which + core - 2 * which * core

    def diagonal(e):
        p = at_row[e]
        for which in range(2):
            put(p, p, which, which, held[e, other(which), at_plane[e]])
            put(p, p, 1 - which, which, held[e, other(which), planes])

    def off_diagonal(e, f):
        up = at_row[e] < at_row[f]
        lo, hi = jnp.where(up, e, f), jnp.where(up, f, e)
        p, q = jnp.where(up, at_row[e], at_row[f]), jnp.where(up, at_row[f], at_row[e])
        p_plane, q_plane = jnp.where(up, at_plane[e], at_plane[f]), jnp.where(up, at_plane[f], at_plane[e])
        for which in range(2):
            upper = held[lo, other(which), q_plane]
            put(p, q, which, which, upper)
            put(q, p, which, which, upper.T)
            lower = held[hi, other(which), p_plane]
            put(q, p, 1 - which, which, lower)
            put(p, q, which, 1 - which, lower.T)

    from_core(OWN)
    diagonal(OWN)
    from_core(ALONG_X)
    diagonal(ALONG_X)
    off_diagonal(OWN, ALONG_X)
    from_pair(ACROSS, 0)
    from_pair(ACROSS, 1)
    to_core(ACROSS, 0)
    from_core(ALONG_Y)
    diagonal(ALONG_Y)
    off_diagonal(OWN, ALONG_Y)
    off_diagonal(ALONG_X, ALONG_Y)
    for s in range(2, planes + 1):
        from_pair(ACROSS, s)
    to_core(ACROSS, 1)
    from_core(ACROSS)
    diagonal(ACROSS)
    for e in (OWN, ALONG_X, ALONG_Y):
        off_diagonal(e, ACROSS)

    same_bytes = total.at[0:sum(sent)]
    pltpu.make_async_copy(same_bytes, same_bytes, send_sem).wait()

    @pl.when(on_diagonal)
    def _():
        for s in range(1, planes):
            extra_to_line(s).wait_send()


def multiply(structure_ref, gram, tri, diag_ref, out_ref, var_ref, result, var, out_sem, var_sem):
    spans = gram.shape[0]
    block = gram.shape[2]
    width = tri.shape[1]
    tile = block
    copies = []

    def send(source, target, sem):
        copies.append(pltpu.make_async_copy(source, target, sem))
        copies[-1].start()

    for n in range(width // tile):
        cols = slice(n * tile, (n + 1) * tile)
        total = jnp.zeros((1, tile), jnp.float32)
        for i in range(spans):
            own = jnp.concatenate([gram[structure_ref[0, i], structure_ref[0, m]] for m in range(spans)], axis=1)
            product = -jnp.dot(own, tri[:, cols], preferred_element_type=jnp.float32)
            result[i * block:(i + 1) * block, cols] = product.astype(jnp.bfloat16)
            total += jnp.sum(tri[i * block:(i + 1) * block, cols].astype(jnp.float32) * product, axis=0, keepdims=True)
        var[:, cols] = diag_ref[:, cols] - total
        send(result.at[:, cols], out_ref.at[:, cols], out_sem.at[n])
    send(var, var_ref, var_sem)
    for copy in copies:
        copy.wait()


def gathered(planes, sigma_anc, structure, factor, diag_term):
    rows, half = sigma_anc.shape
    spans = structure.shape[1]
    depth, width = factor.shape[1:]
    anywhere = pl.BlockSpec(memory_space=pl.ANY)
    in_hbm = pl.BlockSpec(memory_space=pltpu.HBM)
    in_vmem = pl.BlockSpec(memory_space=pltpu.VMEM)
    in_smem = pl.BlockSpec(memory_space=pltpu.SMEM)
    dma = pltpu.SemaphoreType.DMA
    pieces = spans * 2 * (planes + 1)
    gram = pl.pallas_call(
        functools.partial(kernel, planes),
        out_shape=jax.ShapeDtypeStruct((spans, spans, 2 * half, 2 * half), jnp.bfloat16),
        in_specs=[in_hbm],
        out_specs=in_vmem,
        scratch_shapes=[
            pltpu.VMEM((spans, 2, planes + 1, half, half), jnp.bfloat16),
            pltpu.VMEM((pieces, half, half), jnp.bfloat16),
            dma((2,)),
            dma(()),
            dma((planes,)),
            dma((planes,)),
            dma((spans, planes + 1)),
            dma((spans, 2)),
        ],
        compiler_params=pltpu.CompilerParams(
            collective_id=0, has_side_effects=True, vmem_limit_bytes=16 * 1024 * 1024
        ),
        cost_estimate=pl.CostEstimate(flops=0, bytes_accessed=16 * depth * depth, transcendentals=0),
    )(pltpu.with_memory_space_constraint(sigma_anc, pltpu.HBM))
    off, variance = pl.pallas_call(
        multiply,
        out_shape=(
            jax.ShapeDtypeStruct((depth, width), jnp.bfloat16),
            jax.ShapeDtypeStruct((1, width), jnp.float32),
        ),
        in_specs=[in_smem, in_vmem, in_vmem, in_vmem],
        out_specs=(anywhere, anywhere),
        scratch_shapes=[
            pltpu.VMEM((depth, width), jnp.bfloat16),
            pltpu.VMEM((1, width), jnp.float32),
            dma((width // (depth // spans),)),
            dma(()),
        ],
        compiler_params=pltpu.CompilerParams(vmem_limit_bytes=24 * 1024 * 1024),
        cost_estimate=pl.CostEstimate(
            flops=2 * depth * depth * width, bytes_accessed=4 * depth * width, transcendentals=0
        ),
    )(structure, gram, factor[0], diag_term)
    return off[None], variance


def selected(sigma_anc, structure, factor, diag_term):
    span_count = structure.shape[1]
    block_rows = factor.shape[1] // span_count
    own_blocks = structure[0]
    triangle = factor[0]
    panel = lax.all_gather(sigma_anc, "col", axis=1, tiled=True)
    structures = lax.all_gather(structure, "row", axis=0, tiled=True)
    block_total = panel.shape[1] // block_rows
    blocked = panel.reshape(block_rows, block_total, block_rows)
    outgoing = jnp.take(blocked, structures, axis=1)
    outgoing = outgoing.reshape(block_rows, structures.shape[0], span_count * block_rows)
    received = lax.all_to_all(outgoing, "row", split_axis=1, concat_axis=1, tiled=True)
    picked = jnp.take(received, own_blocks, axis=1)
    product = jnp.einsum("bim,mw->ibw", picked, triangle, preferred_element_type=jnp.float32)
    off_block = -product.reshape(span_count * block_rows, triangle.shape[1])
    variance = diag_term[0] - jnp.sum(triangle.astype(jnp.float32) * off_block, axis=0)
    return (off_block.astype(jnp.bfloat16)[None], variance[None])


def solution(mesh):
    rows, planes = mesh.shape["row"], mesh.shape["col"] // 2

    def body(sigma_anc, structure, factor, diag_term):
        spans = structure.shape[1]
        if rows == spans == planes == ACROSS + 1 and sigma_anc.shape[0] == 2 * sigma_anc.shape[1]:
            return gathered(planes, sigma_anc, structure, factor, diag_term)
        return selected(sigma_anc, structure, factor, diag_term)

    return jax.shard_map(
        body,
        mesh=mesh,
        in_specs=(
            P("row", "col"),
            P(("row", "col"), None),
            P(("row", "col"), None, None),
            P(("row", "col"), None),
        ),
        out_specs=(P(("row", "col"), None, None), P(("row", "col"), None)),
        check_vma=False,
    )
```

```python
import functools

import jax
import jax.numpy as jnp
from jax import lax
from jax.experimental import pallas as pl
from jax.experimental.pallas import tpu as pltpu
from jax.sharding import PartitionSpec as P

MESH = pl.DeviceIdType.MESH
OWN, ALONG_X, ALONG_Y, ACROSS = range(4)


def flip(value, mask):
    bit = 1
    while bit <= mask:
        if mask & bit:
            value = value + bit - 2 * bit * ((value // bit) % 2)
        bit *= 2
    return value


def kernel(
    planes,
    sigma_ref,
    gram,
    held,
    total,
    local_sem,
    send_sem,
    extra_sem,
    line_sem,
    pair_sem,
    core_sem,
):
    row = lax.axis_index("row")
    col = lax.axis_index("col")
    plane, core = col // 2, col % 2
    half = sigma_ref.shape[1]
    spans = gram.shape[0]

    def take(h):
        return sigma_ref.at[pl.ds(pl.multiple_of(h * half, half), half)]

    main = take(jnp.where(row > plane, 1 - core, core))
    extra = take(1 - core)
    on_diagonal = row == plane

    keep = pltpu.make_async_copy(main, held.at[0, 0, 0], local_sem.at[0])
    keep_extra = pltpu.make_async_copy(extra, held.at[0, 0, planes], local_sem.at[1])
    keep.start()
    pl.when(on_diagonal)(keep_extra.start)

    sibling = (row, col + 1 - 2 * core)
    beside = {e: (flip(row, e), col) for e in (ALONG_X, ALONG_Y)}
    line = {s: (row, flip(plane, s) * 2 + core) for s in range(1, planes)}
    greeted = [*line.values(), *beside.values(), sibling]
    barrier = pltpu.get_barrier_semaphore()
    for device in greeted:
        pl.semaphore_signal(barrier, inc=1, device_id=device, device_id_type=MESH)
    pl.semaphore_wait(barrier, len(greeted))

    sent = []

    def remote(source, target, recv, device, send=send_sem):
        return pltpu.make_async_remote_copy(
            src_ref=source, dst_ref=target, send_sem=send, recv_sem=recv,
            device_id=device, device_id_type=MESH)

    def to_line(s):
        remote(main, held.at[0, 0, s], line_sem.at[s], line[s]).start()
        sent.append(1)

    def from_line(s):
        remote(held.at[0, 0, s], held.at[0, 0, s], line_sem.at[s], line[1]).wait_recv()

    def extra_to_line(s):
        return remote(extra, held.at[0, 0, planes], line_sem.at[0], line[s], extra_sem.at[s])

    def to_pair(e, via, s, source=None):
        source = held.at[e, 0, s] if source is None else source
        remote(source, held.at[e + via, 0, s], pair_sem.at[e + via, s], beside[via]).start()
        sent.append(1)

    def from_pair(e, s):
        remote(held.at[e, 0, s], held.at[e, 0, s], pair_sem.at[e, s], beside[ALONG_X]).wait_recv()

    parts = ((0, 2), (2, planes + 1))

    def to_core(e, part):
        lo, hi = parts[part]
        remote(held.at[e, 0, lo:hi], held.at[e, 1, lo:hi], core_sem.at[e, part], sibling).start()
        sent.append(hi - lo)

    def from_core(e):
        for part, (lo, hi) in enumerate(parts):
            remote(held.at[e, 1, lo:hi], held.at[e, 1, lo:hi], core_sem.at[e, part], sibling).wait_recv()

    to_pair(OWN, ALONG_X, 0, main)
    to_pair(OWN, ALONG_Y, 0, main)
    for s in range(1, planes):
        to_line(s)

    @pl.when(on_diagonal)
    def _():
        for s in range(1, planes):
            extra_to_line(s).start()

    keep.wait()
    for s in range(1, planes):
        from_line(s)
        to_pair(OWN, ALONG_X, s)
        to_pair(OWN, ALONG_Y, s)
        if s == 1:
            to_core(OWN, 0)
            from_pair(ALONG_X, 0)
            to_pair(ALONG_X, ALONG_Y, 0)
            from_pair(ALONG_Y, 0)

    @pl.when(on_diagonal)
    def _():
        keep_extra.wait()

    @pl.when(jnp.logical_not(on_diagonal))
    def _():
        extra_to_line(1).wait_recv()

    to_pair(OWN, ALONG_X, planes)
    to_pair(OWN, ALONG_Y, planes)
    to_core(OWN, 1)
    for s in range(1, planes + 1):
        from_pair(ALONG_X, s)
        if s == planes:
            to_pair(ALONG_X, ALONG_Y, s)
        from_pair(ALONG_Y, s)
        if s < planes:
            to_pair(ALONG_Y, ALONG_X, s)
        if s == 1:
            to_core(ALONG_X, 0)
            to_core(ALONG_Y, 0)
    to_core(ALONG_X, 1)
    to_core(ALONG_Y, 1)

    differ, bit = 0, 1
    while bit < planes:
        one, two = (row // bit) % 2, (plane // bit) % 2
        differ = differ + bit * (one + two - 2 * one * two)
        bit *= 2
    at_row = [flip(row, e) for e in range(spans)]
    at_plane = [flip(differ, e) for e in range(spans)]

    def put(p, q, a, b, value):
        gram[p, q, a * half:(a + 1) * half, b * half:(b + 1) * half] = value

    def other(which):
        return which + core - 2 * which * core

    def diagonal(e):
        p = at_row[e]
        for which in range(2):
            put(p, p, which, which, held[e, other(which), at_plane[e]])
            put(p, p, 1 - which, which, held[e, other(which), planes])

    def off_diagonal(e, f):
        up = at_row[e] < at_row[f]
        lo, hi = jnp.where(up, e, f), jnp.where(up, f, e)
        p, q = jnp.where(up, at_row[e], at_row[f]), jnp.where(up, at_row[f], at_row[e])
        p_plane, q_plane = jnp.where(up, at_plane[e], at_plane[f]), jnp.where(up, at_plane[f], at_plane[e])
        for which in range(2):
            upper = held[lo, other(which), q_plane]
            put(p, q, which, which, upper)
            put(q, p, which, which, upper.T)
            lower = held[hi, other(which), p_plane]
            put(q, p, 1 - which, which, lower)
            put(p, q, which, 1 - which, lower.T)

    from_core(OWN)
    diagonal(OWN)
    from_core(ALONG_X)
    diagonal(ALONG_X)
    off_diagonal(OWN, ALONG_X)
    from_pair(ACROSS, 0)
    from_pair(ACROSS, 1)
    to_core(ACROSS, 0)
    for s in range(2, planes + 1):
        from_pair(ACROSS, s)
    to_core(ACROSS, 1)
    from_core(ALONG_Y)
    diagonal(ALONG_Y)
    off_diagonal(OWN, ALONG_Y)
    off_diagonal(ALONG_X, ALONG_Y)
    from_core(ACROSS)
    diagonal(ACROSS)
    for e in (OWN, ALONG_X, ALONG_Y):
        off_diagonal(e, ACROSS)

    same_bytes = total.at[0:sum(sent)]
    pltpu.make_async_copy(same_bytes, same_bytes, send_sem).wait()

    @pl.when(on_diagonal)
    def _():
        for s in range(1, planes):
            extra_to_line(s).wait_send()


def multiply(structure_ref, gram, tri, diag_ref, out_ref, var_ref, result, var, out_sem, var_sem):
    spans = gram.shape[0]
    block = gram.shape[2]
    width = tri.shape[1]
    tile = block
    copies = []

    def send(source, target, sem):
        copies.append(pltpu.make_async_copy(source, target, sem))
        copies[-1].start()

    for n in range(width // tile):
        cols = slice(n * tile, (n + 1) * tile)
        total = jnp.zeros((1, tile), jnp.float32)
        for i in range(spans):
            own = jnp.concatenate([gram[structure_ref[0, i], structure_ref[0, m]] for m in range(spans)], axis=1)
            product = -jnp.dot(own, tri[:, cols], preferred_element_type=jnp.float32)
            result[i * block:(i + 1) * block, cols] = product.astype(jnp.bfloat16)
            total += jnp.sum(tri[i * block:(i + 1) * block, cols].astype(jnp.float32) * product, axis=0, keepdims=True)
        var[:, cols] = diag_ref[:, cols] - total
        send(result.at[:, cols], out_ref.at[:, cols], out_sem.at[n])
    send(var, var_ref, var_sem)
    for copy in copies:
        copy.wait()


def gathered(planes, sigma_anc, structure, factor, diag_term):
    rows, half = sigma_anc.shape
    spans = structure.shape[1]
    depth, width = factor.shape[1:]
    anywhere = pl.BlockSpec(memory_space=pl.ANY)
    in_hbm = pl.BlockSpec(memory_space=pltpu.HBM)
    in_vmem = pl.BlockSpec(memory_space=pltpu.VMEM)
    in_smem = pl.BlockSpec(memory_space=pltpu.SMEM)
    dma = pltpu.SemaphoreType.DMA
    pieces = spans * 2 * (planes + 1)
    gram = pl.pallas_call(
        functools.partial(kernel, planes),
        out_shape=jax.ShapeDtypeStruct((spans, spans, 2 * half, 2 * half), jnp.bfloat16),
        in_specs=[in_hbm],
        out_specs=in_vmem,
        scratch_shapes=[
            pltpu.VMEM((spans, 2, planes + 1, half, half), jnp.bfloat16),
            pltpu.VMEM((pieces, half, half), jnp.bfloat16),
            dma((2,)),
            dma(()),
            dma((planes,)),
            dma((planes,)),
            dma((spans, planes + 1)),
            dma((spans, 2)),
        ],
        compiler_params=pltpu.CompilerParams(
            collective_id=0, has_side_effects=True, vmem_limit_bytes=16 * 1024 * 1024
        ),
        cost_estimate=pl.CostEstimate(flops=0, bytes_accessed=16 * depth * depth, transcendentals=0),
    )(pltpu.with_memory_space_constraint(sigma_anc, pltpu.HBM))
    off, variance = pl.pallas_call(
        multiply,
        out_shape=(
            jax.ShapeDtypeStruct((depth, width), jnp.bfloat16),
            jax.ShapeDtypeStruct((1, width), jnp.float32),
        ),
        in_specs=[in_smem, in_vmem, in_vmem, in_vmem],
        out_specs=(anywhere, anywhere),
        scratch_shapes=[
            pltpu.VMEM((depth, width), jnp.bfloat16),
            pltpu.VMEM((1, width), jnp.float32),
            dma((width // (depth // spans),)),
            dma(()),
        ],
        compiler_params=pltpu.CompilerParams(vmem_limit_bytes=24 * 1024 * 1024),
        cost_estimate=pl.CostEstimate(
            flops=2 * depth * depth * width, bytes_accessed=4 * depth * width, transcendentals=0
        ),
    )(structure, gram, factor[0], diag_term)
    return off[None], variance


def selected(sigma_anc, structure, factor, diag_term):
    span_count = structure.shape[1]
    block_rows = factor.shape[1] // span_count
    own_blocks = structure[0]
    triangle = factor[0]
    panel = lax.all_gather(sigma_anc, "col", axis=1, tiled=True)
    structures = lax.all_gather(structure, "row", axis=0, tiled=True)
    block_total = panel.shape[1] // block_rows
    blocked = panel.reshape(block_rows, block_total, block_rows)
    outgoing = jnp.take(blocked, structures, axis=1)
    outgoing = outgoing.reshape(block_rows, structures.shape[0], span_count * block_rows)
    received = lax.all_to_all(outgoing, "row", split_axis=1, concat_axis=1, tiled=True)
    picked = jnp.take(received, own_blocks, axis=1)
    product = jnp.einsum("bim,mw->ibw", picked, triangle, preferred_element_type=jnp.float32)
    off_block = -product.reshape(span_count * block_rows, triangle.shape[1])
    variance = diag_term[0] - jnp.sum(triangle.astype(jnp.float32) * off_block, axis=0)
    return (off_block.astype(jnp.bfloat16)[None], variance[None])


def solution(mesh):
    rows, planes = mesh.shape["row"], mesh.shape["col"] // 2

    def body(sigma_anc, structure, factor, diag_term):
        spans = structure.shape[1]
        if rows == spans == planes == ACROSS + 1 and sigma_anc.shape[0] == 2 * sigma_anc.shape[1]:
            return gathered(planes, sigma_anc, structure, factor, diag_term)
        return selected(sigma_anc, structure, factor, diag_term)

    return jax.shard_map(
        body,
        mesh=mesh,
        in_specs=(
            P("row", "col"),
            P(("row", "col"), None),
            P(("row", "col"), None, None),
            P(("row", "col"), None),
        ),
        out_specs=(P(("row", "col"), None, None), P(("row", "col"), None)),
        check_vma=False,
    )
```
